32 devices in a mesh: fsdp: 4 (over z), ctx: 4 (over y, x), tp: 2 (over core).
Axes of the slice: x: 2, y: 2, z: 4, core: 2. Of those that a mesh axis runs over, the one named last changes fastest.
Arguments:
- inputs: bfloat16 [4, 1024, 2048], P('fsdp', 'ctx'), may hold values from -6 to 6
- segments: int32 [4, 1024], P('fsdp', 'ctx'), may hold values from 0 to 128, as said below
- positions: int32 [4, 1024], P('fsdp', 'ctx'), may hold values from 0 to 767, as said below
- norm_gain: bfloat16 [2048], P(('fsdp', 'ctx')), may hold values from 0.099609375 to 1.8984375
- query_weight: bfloat16 [2048, 2048], P(('fsdp', 'ctx'), 'tp'), may hold values from -0.125 to 0.125
- key_weight: bfloat16 [2048, 2048], P(('fsdp', 'ctx'), 'tp'), may hold values from -0.125 to 0.125
- value_weight: bfloat16 [2048, 2048], P(('fsdp', 'ctx'), 'tp'), may hold values from -0.125 to 0.125
- out_weight: bfloat16 [2048, 2048], P('tp', ('fsdp', 'ctx')), may hold values from -0.5 to 0.5
- lambdas: float32 [4, 128], replicated, may hold values from -0.8 to 0.8
- head_gain: float32 [256], replicated, may hold values from 0.1 to 1.9
- ffn_gain: bfloat16 [2048], P(('fsdp', 'ctx')), may hold values from 0.099609375 to 1.8984375
- gate_weight: bfloat16 [2048, 5632], P(('fsdp', 'ctx'), 'tp'), may hold values from -0.125 to 0.125
- up_weight: bfloat16 [2048, 5632], P(('fsdp', 'ctx'), 'tp'), may hold values from -0.125 to 0.125
- down_weight: bfloat16 [5632, 2048], P('tp', ('fsdp', 'ctx')), may hold values from -0.078125 to 0.078125
- cotangent: bfloat16 [4, 1024, 2048], P('fsdp', 'ctx'), may hold values from -6 to 6
Outputs:
- output: bfloat16 [4, 1024, 2048], P('fsdp', 'ctx')
- grad_input: bfloat16 [4, 1024, 2048], P('fsdp', 'ctx')
- grad_norm_gain: float32 [2048], P(('fsdp', 'ctx'))
- grad_query: float32 [2048, 2048], P(('fsdp', 'ctx'), 'tp')
- grad_key: float32 [2048, 2048], P(('fsdp', 'ctx'), 'tp')
- grad_value: float32 [2048, 2048], P(('fsdp', 'ctx'), 'tp')
- grad_out: float32 [2048, 2048], P('tp', ('fsdp', 'ctx'))
- grad_lambdas: float32 [4, 128], replicated
- grad_head_gain: float32 [256], replicated
- grad_ffn_gain: float32 [2048], P(('fsdp', 'ctx'))
- grad_gate: float32 [2048, 5632], P(('fsdp', 'ctx'), 'tp')
- grad_up: float32 [2048, 5632], P(('fsdp', 'ctx'), 'tp')
- grad_down: float32 [5632, 2048], P('tp', ('fsdp', 'ctx'))
The draws below stay inside these ranges and needn't reach their ends.
Inputs may be any that keep to these rules, and one draw needn't show every extreme that they name: `segments`: within a row, document numbers start at 0, never fall along the row, and rise by at most one from a token to the next. `positions`: each token's position within its document: 0 at a document's first token, one more at each further token of it.
All inputs are finite; a program needn't handle non-finite values.
Results may differ from the reference program's by a relative error of at most 0.025.
Values may be sent and summed in bfloat16 or wider, within the bound.
No kernel may reach another device: no remote copies, remote signals or barrier semaphores. Data moves between devices by JAX's collectives and lax.ppermute only.
A program may use at most 256 MiB of HBM per device.

```python
import math
import jax
import jax.numpy as jnp
from jax import lax

D = 2048
HEADS = 8
QK = 128
VD = 256
FF = 5632
TOK_DEV = 256
LENGTH = 1024
ROWS = 4


def document_layout(key):
    head_key, tail_key = jax.random.split(key, 2)
    halfway = TOK_DEV // 2
    slots = halfway - 1
    chosen = slots // 2
    opening = halfway
    closing = LENGTH - halfway
    places = jnp.arange(LENGTH, dtype=jnp.int32)[None, :]

    def pick(row_key):
        return jax.random.permutation(row_key, slots) < chosen
    pieces = [jnp.zeros((ROWS, 1), dtype=bool)]
    if slots > 0:
        pieces.append(jax.vmap(pick)(jax.random.split(head_key, ROWS)))
    pieces.append(jnp.ones((ROWS, 1), dtype=bool))
    pieces.append(jnp.zeros((ROWS, closing - opening - 1), dtype=bool))
    pieces.append(jnp.ones((ROWS, 1), dtype=bool))
    if slots > 0:
        pieces.append(jax.vmap(pick)(jax.random.split(tail_key, ROWS)))
    breaks = jnp.concatenate(pieces, axis=1)
    segment_ids = jnp.cumsum(breaks.astype(jnp.int32), axis=1)
    starts = lax.cummax(jnp.where(breaks, places, 0), axis=1)
    return (segment_ids.astype(jnp.int32), (places - starts).astype(jnp.int32))


def draw_segments(key, part):
    return document_layout(key)[0]


def draw_positions(key, part):
    return document_layout(key)[1]


def block_levels(stream_key, extent, shards, low, high):
    def one(axis_at, parts):
        draws = jax.random.uniform(jax.random.fold_in(jax.random.fold_in(stream_key, 6), axis_at), (parts,), jnp.float32, low / len(shards), high / len(shards))
        return jnp.repeat(jnp.exp(draws), extent[axis_at] // parts).reshape((-1,) + (1,) * (len(extent) - axis_at - 1))

    level = one(*shards[0])
    for cut in shards[1:]:
        level = level * one(*cut)
    return level


def noise(rng, extent, scale, bound, cuts=(), kind=jnp.bfloat16):
    factor_of = block_levels(rng, extent, cuts, -0.22, 0.18) if cuts else 1.0
    values = jax.random.normal(rng, extent, jnp.float32) * scale * factor_of
    return jnp.minimum(jnp.maximum(values, -bound), bound).astype(kind)


def setup_inputs(seed: int = 0) -> dict:
    arg_keys = jax.random.split(jax.random.key(seed), 16)
    return {
        "inputs": noise(arg_keys[0], (ROWS, LENGTH, D), 1.0, 6.0, ((0, 4), (1, 4))),
        "segments": draw_segments(jax.random.fold_in(arg_keys[15], 71), 0),
        "positions": draw_positions(jax.random.fold_in(arg_keys[15], 71), 0),
        "norm_gain": jnp.clip(1.0 + 0.18 * jax.random.normal(arg_keys[3], (D,), jnp.float32), 0.099609375, 1.8984375).astype(jnp.bfloat16),
        "query_weight": noise(arg_keys[4], (D, HEADS * 2 * QK), D ** -0.5, 0.125, ((0, 16), (1, 2))),
        "key_weight": noise(arg_keys[5], (D, HEADS * 2 * QK), D ** -0.5, 0.125, ((0, 16), (1, 2))),
        "value_weight": noise(arg_keys[6], (D, HEADS * VD), D ** -0.5, 0.125, ((0, 16), (1, 2))),
        "out_weight": noise(arg_keys[7], (HEADS * VD, D), (HEADS * VD // 16) ** -0.5, 0.5, ((0, 2), (1, 16))),
        "lambdas": noise(arg_keys[8], (4, QK), 0.2, 0.8, (), jnp.float32),
        "head_gain": jnp.clip(1.0 + 0.18 * jax.random.normal(arg_keys[9], (VD,), jnp.float32), 0.1, 1.9),
        "ffn_gain": jnp.clip(1.0 + 0.18 * jax.random.normal(arg_keys[10], (D,), jnp.float32), 0.099609375, 1.8984375).astype(jnp.bfloat16),
        "gate_weight": noise(arg_keys[11], (D, FF), D ** -0.5, 0.125, ((0, 16), (1, 2))),
        "up_weight": noise(arg_keys[12], (D, FF), D ** -0.5, 0.125, ((0, 16), (1, 2))),
        "down_weight": noise(arg_keys[13], (FF, D), FF ** -0.5, 0.078125, ((0, 2), (1, 16))),
        "cotangent": noise(arg_keys[14], (ROWS, LENGTH, D), 1.0, 6.0, ((0, 4), (1, 4))),
    }


epsilon = 1e-05
rope_base = 10000.0
lambda_init = 0.8 - 0.6 * math.exp(-1.8)
masked_score = -1e+30

@jax.custom_vjp
def low(v):
    return lax.optimization_barrier(v.astype(jnp.bfloat16)).astype(jnp.float32)

@jax.custom_vjp
def low_back(v):
    return v

def low_keep(v):
    return (low(v), None)

def low_pass(kept, grad):
    return (grad,)

def back_keep(v):
    return (v, None)

def back_low(kept, grad):
    return (low(grad),)
low.defvjp(low_keep, low_pass)
low_back.defvjp(back_keep, back_low)

def matmul(left, right):
    return jnp.matmul(left, right, precision=lax.Precision.HIGHEST)

def normalize(values):
    return values * lax.rsqrt(lax.optimization_barrier(jnp.mean(values * values, axis=-1, keepdims=True)) + epsilon)

def rotary_tables(positions):
    halfway = QK // 2
    spacing = jnp.arange(halfway, dtype=jnp.float32) * (2.0 / QK)
    frequency = jnp.exp(-math.log(rope_base) * spacing)
    angles = positions.astype(jnp.float32)[..., None] * frequency
    cosine = jnp.concatenate([jnp.cos(angles), jnp.cos(angles)], axis=-1)
    sine_table = jnp.concatenate([jnp.sin(angles), jnp.sin(angles)], axis=-1)
    return (cosine, sine_table)

def rotate(values, cosine, sine_table):
    halfway = values.shape[-1] // 2
    turned = jnp.concatenate([-values[..., halfway:], values[..., :halfway]], axis=-1)
    return values * cosine + turned * sine_table

def row_attention(queries, all_keys, values, segment_row, weight_lambda):
    block_rows = min(512, LENGTH)
    block_count = LENGTH // block_rows
    places = jnp.arange(LENGTH, dtype=jnp.int32)
    scaling = 1.0 / math.sqrt(QK)

    def one_block(inputs):
        query_block, segment_block, place_block = inputs
        scores = jnp.einsum('thmd,khmd->hmtk', query_block, all_keys, precision=lax.Precision.HIGHEST) * scaling
        scores = low_back(scores)
        allowed = (segment_block[:, None] == segment_row[None, :]) & (places[None, :] <= place_block[:, None])
        allowed = allowed[None, None]
        masked = jnp.where(allowed, scores, masked_score)
        largest = lax.optimization_barrier(jnp.max(masked, axis=-1, keepdims=True))
        exponent = jnp.where(allowed, jnp.exp(masked - largest), 0.0)
        shares = exponent / lax.optimization_barrier(jnp.sum(exponent, axis=-1, keepdims=True))
        weights = low(shares[:, 0] - weight_lambda * shares[:, 1])
        return jnp.einsum('htk,khv->thv', weights, values, precision=lax.Precision.HIGHEST)
    outputs = lax.map(jax.checkpoint(one_block), (queries.reshape(block_count, block_rows, HEADS, 2, QK), segment_row.reshape(block_count, block_rows), places.reshape(block_count, block_rows)))
    return outputs.reshape(LENGTH, HEADS, VD)

def reference(inputs, segments, positions, norm_gain, query_weight, key_weight, value_weight, out_weight, lambdas, head_gain, ffn_gain, gate_weight, up_weight, down_weight, cotangent):
    cosine, sine_table = rotary_tables(positions)
    cosine = cosine[:, :, None, None, :]
    sine_table = sine_table[:, :, None, None, :]

    def forward(hidden_in, gain_one, query_full, key_full, value_full, out_full, lambda_rows, gain_head, gain_two, gate_full, up_full, down_full):
        normed_one = low(normalize(hidden_in) * gain_one)
        query_pre = low_back(matmul(normed_one, query_full)).reshape(ROWS, LENGTH, HEADS, 2, QK)
        key_pre = low_back(matmul(normed_one, key_full)).reshape(ROWS, LENGTH, HEADS, 2, QK)
        value_rows = low(low_back(matmul(normed_one, value_full))).reshape(ROWS, LENGTH, HEADS, VD)
        query_rot = low(rotate(query_pre, cosine, sine_table))
        key_rot = low(rotate(key_pre, cosine, sine_table))
        weight_lambda = jnp.exp(jnp.sum(lambda_rows[0] * lambda_rows[1])) - jnp.exp(jnp.sum(lambda_rows[2] * lambda_rows[3])) + lambda_init

        def one_row(row_inputs):
            return row_attention(row_inputs[0], row_inputs[1], row_inputs[2], row_inputs[3], weight_lambda)
        attended = lax.map(one_row, (query_rot, key_rot, value_rows, segments))
        attended = low_back(attended)
        headed = low(normalize(attended) * gain_head * (1.0 - lambda_init)).reshape(ROWS, LENGTH, HEADS * VD)
        branch = low_back(matmul(headed, out_full))
        middle = hidden_in + branch
        normed_two = low(normalize(middle) * gain_two)
        gate_rows = low_back(matmul(normed_two, gate_full))
        upward = low_back(matmul(normed_two, up_full))
        hidden_units = low(jax.nn.silu(gate_rows) * upward)
        return middle + matmul(hidden_units, down_full)
    operands = [operand.astype(jnp.float32) for operand in (inputs, norm_gain, query_weight, key_weight, value_weight, out_weight, lambdas, head_gain, ffn_gain, gate_weight, up_weight, down_weight)]
    result, pullback = jax.vjp(forward, *operands)
    grads = pullback(cotangent.astype(jnp.float32))
    return (result.astype(jnp.bfloat16), grads[0].astype(jnp.bfloat16), grads[1], grads[2], grads[3], grads[4], grads[5], grads[6], grads[7], grads[8], grads[9], grads[10], grads[11])
```

```python
import math

import jax
import jax.numpy as jnp
from jax import lax
from jax.sharding import PartitionSpec as P

epsilon = 1e-05
rope_base = 10000.0
lambda_init = 0.8 - 0.6 * math.exp(-1.8)
masked_score = -1e30


def cut_along(array, dim, count):
    before, after = (array.shape[:dim], array.shape[dim + 1 :])
    return jnp.moveaxis(array.reshape(*before, count, -1, *after), dim, 0)


def sum_at_owner(array, axis, dim):
    blocks = cut_along(array, dim, lax.axis_size(axis))
    arrived = lax.all_to_all(blocks, axis, split_axis=0, concat_axis=0, tiled=True)
    return arrived.astype(jnp.float32).sum(axis=0)


def side_by_side(arrays, axis, dim, along):
    columns = [a.reshape(*a.shape[:along], -1) for a in arrays]
    both = jnp.concatenate(columns, axis=along)
    whole, at, finished = (sum_at_owner(both, axis, dim), 0, [])
    for a, column in zip(arrays, columns):
        slab = whole[..., at : at + column.shape[along]]
        finished.append(slab.reshape(*slab.shape[:along], *a.shape[along:]))
        at += column.shape[along]
    return tuple(finished)


def rotary_tables(positions, width):
    halfway = width // 2
    spacing = jnp.arange(halfway, dtype=jnp.float32) * (2.0 / width)
    frequency = jnp.exp(-math.log(rope_base) * spacing)
    angles = positions.astype(jnp.float32)[..., None] * frequency
    cosine = jnp.concatenate([jnp.cos(angles), jnp.cos(angles)], axis=-1)
    sine_table = jnp.concatenate([jnp.sin(angles), jnp.sin(angles)], axis=-1)
    return (cosine[:, None, None, :], sine_table[:, None, None, :])


def rotate(values, cosine, sine_table):
    halfway = values.shape[-1] // 2
    turned = jnp.concatenate([-values[..., halfway:], values[..., :halfway]], axis=-1)
    return values * cosine + turned * sine_table


def normalize(values):
    inverse = lax.rsqrt(jnp.mean(values * values, axis=-1, keepdims=True) + epsilon)
    return (values * inverse, inverse)


def normalize_back(grad_unit, unit_rows, inverse):
    return inverse * (
        grad_unit - unit_rows * jnp.mean(grad_unit * unit_rows, axis=-1, keepdims=True)
    )


def tensor_total(part_sum):
    return lax.psum(part_sum, "tp")


def fetch_attention(norm_gain, query_weight, key_weight, value_weight, out_weight):
    row_parts = (
        lax.all_gather(norm_gain, ("fsdp", "ctx"), axis=0, tiled=True),
        lax.all_gather(query_weight, ("fsdp", "ctx"), axis=0, tiled=True),
        lax.all_gather(key_weight, ("fsdp", "ctx"), axis=0, tiled=True),
        lax.all_gather(value_weight, ("fsdp", "ctx"), axis=0, tiled=True),
    )
    columns = lax.all_gather(out_weight, ("fsdp", "ctx"), axis=1, tiled=True)
    return (row_parts, columns)


def fetch_ffn(ffn_gain, gate_weight, up_weight, down_weight):
    row_parts = (
        lax.all_gather(ffn_gain, ("fsdp", "ctx"), axis=0, tiled=True),
        lax.all_gather(gate_weight, ("fsdp", "ctx"), axis=0, tiled=True),
        lax.all_gather(up_weight, ("fsdp", "ctx"), axis=0, tiled=True),
    )
    columns = lax.all_gather(down_weight, ("fsdp", "ctx"), axis=1, tiled=True)
    return (row_parts, columns)


def shards(
    inputs,
    segments,
    positions,
    norm_gain,
    query_weight,
    key_weight,
    value_weight,
    out_weight,
    lambdas,
    head_gain,
    ffn_gain,
    gate_weight,
    up_weight,
    down_weight,
    cotangent,
):
    token_count = inputs.shape[1]
    qk_width = lambdas.shape[1]
    value_width = head_gain.shape[0]
    heads_here = value_weight.shape[1] // value_width
    length = token_count * lax.axis_size("ctx")
    block_rows = min(512, length)
    block_count = length // block_rows
    scaling = 1.0 / math.sqrt(qk_width)
    query_places = lax.axis_index("ctx") * token_count + jnp.arange(token_count, dtype=jnp.int32)
    query_seg = segments[0]
    cosine, sine_table = rotary_tables(positions[0], qk_width)
    hidden_in = inputs[0].astype(jnp.float32)
    unit_one, inverse_one = normalize(hidden_in)
    attn_parts, out_full = fetch_attention(
        norm_gain, query_weight, key_weight, value_weight, out_weight
    )
    gain_one, query_full, key_full, value_full = attn_parts
    normed_one = (unit_one * gain_one.astype(jnp.float32)).astype(jnp.bfloat16)
    query_pre = jnp.dot(normed_one, query_full, preferred_element_type=jnp.float32).reshape(
        token_count, heads_here, 2, qk_width
    )
    key_pre = jnp.dot(normed_one, key_full, preferred_element_type=jnp.float32).reshape(
        token_count, heads_here, 2, qk_width
    )
    value_rows = (
        jnp.dot(normed_one, value_full, preferred_element_type=jnp.float32)
        .astype(jnp.bfloat16)
        .reshape(token_count, heads_here, value_width)
    )
    query_rot = rotate(query_pre, cosine, sine_table).astype(jnp.bfloat16)
    key_rot = rotate(key_pre, cosine, sine_table).astype(jnp.bfloat16)
    first_exp = jnp.exp(jnp.sum(lambdas[0] * lambdas[1]))
    second_exp = jnp.exp(jnp.sum(lambdas[2] * lambdas[3]))
    weight_lambda = first_exp - second_exp + lambda_init
    seg_all = lax.all_gather(query_seg, "ctx", axis=0, tiled=True)
    keys_all, values_all = (
        lax.all_gather(key_rot, "ctx", axis=0, tiled=True),
        lax.all_gather(value_rows, "ctx", axis=0, tiled=True),
    )
    all_places = jnp.arange(length, dtype=jnp.int32)
    blocks = (
        keys_all.reshape(block_count, block_rows, heads_here, 2, qk_width),
        values_all.reshape(block_count, block_rows, heads_here, value_width),
        seg_all.reshape(block_count, block_rows),
        all_places.reshape(block_count, block_rows),
    )

    def block_scores(block):
        scores = (
            jnp.einsum("thmd,khmd->hmtk", query_rot, block[0], preferred_element_type=jnp.float32)
            * scaling
        )
        allowed = (query_seg[:, None] == block[2][None, :]) & (
            block[3][None, :] <= query_places[:, None]
        )
        allowed = allowed[None, None]
        return (jnp.where(allowed, scores, masked_score), allowed)

    def stats_step(carry, block):
        largest, total = carry
        masked, allowed = block_scores(block)
        fresh = jnp.maximum(largest, jnp.max(masked, axis=-1))
        total = total * jnp.exp(largest - fresh) + jnp.sum(
            jnp.where(allowed, jnp.exp(masked - fresh[..., None]), 0.0), axis=-1
        )
        return ((fresh, total), None)

    start_max = jnp.full((heads_here, 2, token_count), masked_score, jnp.float32)
    (largest, total), unused = lax.scan(stats_step, (start_max, jnp.zeros_like(start_max)), blocks)
    log_total = largest + jnp.log(total)

    def block_shares(block):
        masked, allowed = block_scores(block)
        shares = jnp.where(allowed, jnp.exp(masked - log_total[..., None]), 0.0)
        mix = (shares[:, 0] - weight_lambda * shares[:, 1]).astype(jnp.bfloat16)
        return (shares, mix)

    def output_step(attended, block):
        shares, mix = block_shares(block)
        return (
            attended
            + jnp.einsum("htk,khv->thv", mix, block[1], preferred_element_type=jnp.float32),
            None,
        )

    attended, unused = lax.scan(
        output_step, jnp.zeros((token_count, heads_here, value_width), jnp.float32), blocks
    )
    unit_head, inverse_head = normalize(attended)
    headed = (
        (unit_head * head_gain * (1.0 - lambda_init))
        .astype(jnp.bfloat16)
        .reshape(token_count, heads_here * value_width)
    )
    middle = hidden_in + tensor_total(jnp.dot(headed, out_full, preferred_element_type=jnp.float32))
    ffn_parts, down_full = fetch_ffn(ffn_gain, gate_weight, up_weight, down_weight)
    gain_two, gate_full, up_full = ffn_parts
    unit_two, inverse_two = normalize(middle)
    normed_two = (unit_two * gain_two.astype(jnp.float32)).astype(jnp.bfloat16)
    gate_rows = jnp.dot(normed_two, gate_full, preferred_element_type=jnp.float32)
    upward = jnp.dot(normed_two, up_full, preferred_element_type=jnp.float32)
    hidden_units = (jax.nn.silu(gate_rows) * upward).astype(jnp.bfloat16)
    result = middle + tensor_total(
        jnp.dot(hidden_units, down_full, preferred_element_type=jnp.float32)
    )
    ffn_parts, down_full = fetch_ffn(ffn_gain, gate_weight, up_weight, down_weight)
    gain_two, gate_full, up_full = ffn_parts
    grad_rows = cotangent[0]
    grad_down_full = jnp.einsum(
        "tf,td->fd", hidden_units, grad_rows, preferred_element_type=jnp.float32
    )
    hidden_grad = jnp.einsum("td,fd->tf", grad_rows, down_full, preferred_element_type=jnp.float32)
    sigmoid = jax.nn.sigmoid(gate_rows)
    gate_low = (hidden_grad * upward * (sigmoid * (1.0 + gate_rows * (1.0 - sigmoid)))).astype(
        jnp.bfloat16
    )
    up_low = (hidden_grad * (gate_rows * sigmoid)).astype(jnp.bfloat16)
    grad_gate_full = jnp.einsum(
        "td,tf->df", normed_two, gate_low, preferred_element_type=jnp.float32
    )
    grad_up_full = jnp.einsum("td,tf->df", normed_two, up_low, preferred_element_type=jnp.float32)
    normed_two_grad = tensor_total(
        jnp.einsum("tf,df->td", gate_low, gate_full, preferred_element_type=jnp.float32)
        + jnp.einsum("tf,df->td", up_low, up_full, preferred_element_type=jnp.float32)
    )
    gain_two_grad = jnp.sum(normed_two_grad * unit_two, axis=0)
    middle_grad = grad_rows.astype(jnp.float32) + normalize_back(
        normed_two_grad * gain_two.astype(jnp.float32), unit_two, inverse_two
    )
    grad_ffn_gain, grad_gate, grad_up = (
        lax.psum_scatter(gain_two_grad, ("fsdp", "ctx"), scatter_dimension=0, tiled=True),
        lax.psum_scatter(grad_gate_full, ("fsdp", "ctx"), scatter_dimension=0, tiled=True),
        lax.psum_scatter(grad_up_full, ("fsdp", "ctx"), scatter_dimension=0, tiled=True),
    )
    grad_down = lax.psum_scatter(grad_down_full, ("fsdp", "ctx"), scatter_dimension=1, tiled=True)
    attn_parts, out_full = fetch_attention(
        norm_gain, query_weight, key_weight, value_weight, out_weight
    )
    gain_one, query_full, key_full, value_full = attn_parts
    branch_grad = middle_grad.astype(jnp.bfloat16)
    grad_out_full = jnp.einsum("tf,td->fd", headed, branch_grad, preferred_element_type=jnp.float32)
    headed_grad = jnp.einsum(
        "td,fd->tf", branch_grad, out_full, preferred_element_type=jnp.float32
    ).reshape(token_count, heads_here, value_width)
    scaled_grad = headed_grad * (1.0 - lambda_init)
    head_gain_grad = jnp.sum(scaled_grad * unit_head, axis=(0, 1))
    attended_grad = normalize_back(scaled_grad * head_gain, unit_head, inverse_head).astype(
        jnp.bfloat16
    )

    def sums_step(carry, block):
        first_sum, second_sum = carry
        shares, mix = block_shares(block)
        mix_grad = jnp.einsum(
            "thv,khv->htk", attended_grad, block[1], preferred_element_type=jnp.float32
        )
        return (
            (
                first_sum + jnp.sum(shares[:, 0] * mix_grad, axis=-1),
                second_sum + jnp.sum(shares[:, 1] * mix_grad, axis=-1),
            ),
            None,
        )

    start_sums = jnp.zeros((heads_here, token_count), jnp.float32)
    (first_sum, second_sum), unused = lax.scan(sums_step, (start_sums, start_sums), blocks)
    query_start = jnp.zeros((token_count, heads_here, 2, qk_width), jnp.float32)

    def grad_step(query_grad, block):
        shares, mix = block_shares(block)
        mix_grad = jnp.einsum(
            "thv,khv->htk", attended_grad, block[1], preferred_element_type=jnp.float32
        )
        score_grad = jnp.stack(
            [
                shares[:, 0] * (mix_grad - first_sum[..., None]),
                -weight_lambda * shares[:, 1] * (mix_grad - second_sum[..., None]),
            ],
            axis=1,
        ).astype(jnp.bfloat16)
        query_grad = query_grad + jnp.einsum(
            "hmtk,khmd->thmd", score_grad, block[0], preferred_element_type=jnp.float32
        )
        key_block_grad = (
            jnp.einsum("hmtk,thmd->khmd", score_grad, query_rot, preferred_element_type=jnp.float32)
            * scaling
        )
        value_block_grad = jnp.einsum(
            "htk,thv->khv", mix, attended_grad, preferred_element_type=jnp.float32
        )
        return (query_grad, (key_block_grad, value_block_grad))

    query_grad, (key_stack, value_stack) = lax.scan(grad_step, query_start, blocks)
    key_back, value_back = (
        lax.psum_scatter(
            key_stack.reshape(length, heads_here, 2, qk_width),
            "ctx",
            scatter_dimension=0,
            tiled=True,
        ),
        lax.psum_scatter(
            value_stack.reshape(length, heads_here, value_width),
            "ctx",
            scatter_dimension=0,
            tiled=True,
        ),
    )
    query_low = (
        rotate(query_grad * scaling, cosine, -sine_table)
        .astype(jnp.bfloat16)
        .reshape(token_count, heads_here * 2 * qk_width)
    )
    key_low = (
        rotate(key_back, cosine, -sine_table)
        .astype(jnp.bfloat16)
        .reshape(token_count, heads_here * 2 * qk_width)
    )
    value_low = value_back.astype(jnp.bfloat16).reshape(token_count, heads_here * value_width)
    grad_query_full = jnp.einsum(
        "td,tf->df", normed_one, query_low, preferred_element_type=jnp.float32
    )
    grad_key_full = jnp.einsum("td,tf->df", normed_one, key_low, preferred_element_type=jnp.float32)
    grad_value_full = jnp.einsum(
        "td,tf->df", normed_one, value_low, preferred_element_type=jnp.float32
    )
    normed_one_part = jnp.einsum(
        "tf,df->td", query_low, query_full, preferred_element_type=jnp.float32
    )
    normed_one_part = normed_one_part + jnp.einsum(
        "tf,df->td", key_low, key_full, preferred_element_type=jnp.float32
    )
    normed_one_part = normed_one_part + jnp.einsum(
        "tf,df->td", value_low, value_full, preferred_element_type=jnp.float32
    )
    normed_one_grad = tensor_total(normed_one_part)
    gain_one_grad = jnp.sum(normed_one_grad * unit_one, axis=0)
    input_grad = middle_grad + normalize_back(
        normed_one_grad * gain_one.astype(jnp.float32), unit_one, inverse_one
    )
    grad_norm_gain, grad_query, grad_key, grad_value = side_by_side(
        (
            gain_one_grad.astype(jnp.bfloat16),
            grad_query_full.astype(jnp.bfloat16),
            grad_key_full.astype(jnp.bfloat16),
            grad_value_full.astype(jnp.bfloat16),
        ),
        ("fsdp", "ctx"),
        0,
        1,
    )
    grad_out = lax.psum_scatter(grad_out_full, ("fsdp", "ctx"), scatter_dimension=1, tiled=True)
    lambda_scalar = -jnp.sum(second_sum)
    lambda_local = lambda_scalar * jnp.stack(
        [
            first_exp * lambdas[1],
            first_exp * lambdas[0],
            -second_exp * lambdas[3],
            -second_exp * lambdas[2],
        ]
    )
    grad_lambdas, grad_head_gain = lax.psum((lambda_local, head_gain_grad), ("fsdp", "ctx", "tp"))
    return (
        result.astype(jnp.bfloat16)[None],
        input_grad.astype(jnp.bfloat16)[None],
        grad_norm_gain,
        grad_query,
        grad_key,
        grad_value,
        grad_out,
        grad_lambdas,
        grad_head_gain,
        grad_ffn_gain,
        grad_gate,
        grad_up,
        grad_down,
    )


heads_total = 8


def fits_by_head(sizes):
    return sizes["ctx"] == 4 and sizes["fsdp"] == 4 and sizes["tp"] == 2


def partner(values, axis, step):
    if step == 0:
        return values
    return lax.ppermute(values, axis, [(i, i ^ step) for i in range(lax.axis_size(axis))])


def partners(values, axis):
    return [partner(values, axis, k) for k in range(lax.axis_size(axis))]


def reorder(blocks, index):
    bit = 1
    while bit < len(blocks):
        flip = (index & bit) != 0
        blocks = [jnp.where(flip, blocks[k ^ bit], blocks[k]) for k in range(len(blocks))]
        bit *= 2
    return blocks


def exchange(blocks, axis):
    index = lax.axis_index(axis)
    sent = reorder(blocks, index)
    return reorder([partner(b, axis, k) for k, b in enumerate(sent)], index)


def sum_partners(blocks, axis):
    total = blocks[0].astype(jnp.float32)
    for k in range(1, len(blocks)):
        total = total + partner(blocks[k], axis, k).astype(jnp.float32)
    return total


def split(values, count, dim):
    return jnp.split(values, count, axis=dim)


def gather_tokens(rows, axis):
    near = jnp.concatenate(partners(rows, axis), axis=0)
    return jnp.concatenate([near, partner(near, "tp", 1)], axis=0)


def scatter_tokens(partial, axis):
    rows = partial.shape[0] // 2
    near = partial[:rows].astype(jnp.float32) + partner(partial[rows:], "tp", 1).astype(jnp.float32)
    return sum_partners(split(near.astype(jnp.bfloat16), lax.axis_size(axis), 0), axis)


def times(left, right):
    return jnp.dot(left, right, preferred_element_type=jnp.float32)


def times_t(left, right):
    return lax.dot_general(left, right, (((1,), (1,)), ((), ())), preferred_element_type=jnp.float32)


def t_times(left, right):
    return lax.dot_general(left, right, (((0,), (0,)), ((), ())), preferred_element_type=jnp.float32)


def sum_times(left, rights):
    parts = split(left, len(rights), 1)
    total = times(parts[0], rights[0])
    for a, b in zip(parts[1:], rights[1:]):
        total = total + times(a, b)
    return total


def by_head(
    inputs,
    segments,
    positions,
    norm_gain,
    query_weight,
    key_weight,
    value_weight,
    out_weight,
    lambdas,
    head_gain,
    ffn_gain,
    gate_weight,
    up_weight,
    down_weight,
    cotangent,
):
    token_count, width = inputs.shape[1], inputs.shape[2]
    half = token_count // 2
    qk_width = lambdas.shape[1]
    value_width = head_gain.shape[0]
    n_z, n_c = lax.axis_size("fsdp"), lax.axis_size("ctx")
    z, c, core = lax.axis_index("fsdp"), lax.axis_index("ctx"), lax.axis_index("tp")
    piece = norm_gain.shape[0]
    scaling = 1.0 / math.sqrt(qk_width)
    bf16, f32 = jnp.bfloat16, jnp.float32

    def plain_to_near(v):
        return jnp.concatenate(reorder(split(v, n_z, 1), z), axis=1)

    def plain_to_ffn(v):
        by_z = [split(b, n_c, 1) for b in split(v, n_z, 1)]
        by_c = [jnp.concatenate([by_z[i][j] for i in range(n_z)], axis=1) for j in range(n_c)]
        return jnp.concatenate(reorder(by_c, c), axis=1)

    def ffn_to_plain(v):
        by_c = [split(b, n_z, 1) for b in reorder(split(v, n_c, 1), c)]
        return jnp.concatenate(
            [by_c[j][i] for i in range(n_z) for j in range(n_c)], axis=1
        )

    def own_half(v):
        return lax.dynamic_slice_in_dim(v, core * half, half, 0)

    small = jnp.concatenate(
        [norm_gain.astype(f32), ffn_gain.astype(f32), segments[0].astype(f32), positions[0].astype(f32)]
    )
    smalls = partners(small, "ctx")
    gains = jnp.stack(reorder([s[: 2 * piece] for s in smalls], c))
    gains = jnp.stack(partners(gains, "fsdp")).reshape(n_z, n_c, 2, piece)
    gain_one = gains[:, :, 0].reshape(1, width)
    gain_two = gains[:, :, 1].reshape(1, width)

    def of_tokens(at):
        both = [
            (s[at : at + half], s[at + half : at + token_count]) for s in smalls
        ]
        first = [jnp.where(core == 0, a, b) for a, b in both]
        second = [jnp.where(core == 0, b, a) for a, b in both]
        return jnp.concatenate(first + second)

    seg_row = of_tokens(2 * piece)
    pos_row = of_tokens(2 * piece + token_count)
    place = jnp.arange(half, dtype=jnp.int32)
    places = jnp.concatenate(
        [(c ^ kc) * token_count + (core ^ kt) * half + place for kt in range(2) for kc in range(n_c)]
    )

    out_t = out_weight.T
    qkv_cols = [
        jnp.concatenate(parts, axis=1)
        for parts in zip(
            split(query_weight, n_c, 1), split(key_weight, n_c, 1), split(value_weight, n_c, 1)
        )
    ]
    qkv_full = partners(jnp.concatenate(exchange(qkv_cols, "ctx"), axis=0), "fsdp")
    out_full = partners(jnp.concatenate(exchange(split(out_t, n_c, 1), "ctx"), axis=0), "fsdp")

    ffn_cols = [
        jnp.concatenate(parts, axis=0)
        for parts in zip(
            split(gate_weight, n_z, 1), split(up_weight, n_z, 1), split(down_weight.T, n_z, 1)
        )
    ]
    units = ffn_cols[0].shape[1]
    ffn_mine = [split(b, 3, 0) for b in exchange(ffn_cols, "fsdp")]
    ffn_mine = jnp.concatenate([b[w] for w in range(3) for b in ffn_mine], axis=0)
    ffn_full = [split(b, 3, 0) for b in partners(ffn_mine, "ctx")]
    gate_full = [b[0] for b in ffn_full]
    up_full = [b[1] for b in ffn_full]
    down_full = [b[2] for b in ffn_full]

    x_own = plain_to_near(own_half(inputs[0]))
    x_all = gather_tokens(x_own, "ctx").astype(f32)
    unit_all, unused = normalize(x_all)
    normed_one = (unit_all * gain_one).astype(bf16)
    hidden_own = x_own.astype(f32)
    unit_one, inverse_one = normalize(hidden_own)
    qkv = sum_times(normed_one, qkv_full)
    query_pre, key_pre = qkv[:, : 2 * qk_width], qkv[:, 2 * qk_width : 4 * qk_width]
    value_rows = qkv[:, 4 * qk_width :].astype(bf16)
    halfway = qk_width // 2
    spacing = jnp.arange(halfway, dtype=f32) * (2.0 / qk_width)
    frequency = jnp.exp(-math.log(rope_base) * spacing)
    angles = pos_row[:, None] * frequency
    cos, sin = jnp.cos(angles), jnp.sin(angles)
    cosine = jnp.concatenate([cos, cos], axis=-1)
    sine = jnp.concatenate([sin, sin], axis=-1)

    def rotate_maps(v, sines):
        return jnp.concatenate(
            [rotate(part, cosine, sines) for part in split(v, 2, 1)], axis=1
        )

    query_rot = rotate_maps(query_pre, sine).astype(bf16)
    key_rot = rotate_maps(key_pre, sine).astype(bf16)
    first_exp = jnp.exp(jnp.sum(lambdas[0] * lambdas[1]))
    second_exp = jnp.exp(jnp.sum(lambdas[2] * lambdas[3]))
    weight_lambda = first_exp - second_exp + lambda_init
    allowed = (seg_row[:, None] == seg_row[None, :]) & (places[None, :] <= places[:, None])

    def shares_of(q, k):
        masked = jnp.where(allowed, times_t(q, k) * scaling, masked_score)
        exponent = jnp.where(
            allowed, jnp.exp(masked - jnp.max(masked, axis=-1, keepdims=True)), 0.0
        )
        return exponent / jnp.sum(exponent, axis=-1, keepdims=True)

    queries, keys = split(query_rot, 2, 1), split(key_rot, 2, 1)
    shares = [shares_of(q, k) for q, k in zip(queries, keys)]
    mix = (shares[0] - weight_lambda * shares[1]).astype(bf16)
    attended = times(mix, value_rows)
    unit_head, inverse_head = normalize(attended)
    headed = (unit_head * head_gain * (1.0 - lambda_init)).astype(bf16)
    branch = jnp.concatenate([times_t(headed, b).astype(bf16) for b in out_full], axis=1)
    middle = hidden_own + scatter_tokens(branch, "ctx")

    def near_to_ffn(v):
        return plain_to_ffn(plain_to_near(v))

    def ffn_to_near(v):
        return plain_to_near(ffn_to_plain(v))

    unit_two, inverse_two = normalize(middle)
    normed_two = gather_tokens(near_to_ffn((unit_two * gain_two).astype(bf16)), "fsdp")
    grad_own = own_half(cotangent[0])
    grad_rows = gather_tokens(plain_to_ffn(grad_own), "fsdp")
    gate_rows = sum_times(normed_two, gate_full)
    upward = sum_times(normed_two, up_full)
    sigmoid = jax.nn.sigmoid(gate_rows)
    hidden_units = (gate_rows * sigmoid * upward).astype(bf16)
    ffn_out = jnp.concatenate([times_t(hidden_units, b).astype(bf16) for b in down_full], axis=1)
    result = (plain_to_near(middle) + ffn_to_plain(scatter_tokens(ffn_out, "fsdp"))).astype(bf16)

    hidden_grad = sum_times(grad_rows, down_full)
    gate_low = (hidden_grad * upward * (sigmoid * (1.0 + gate_rows * (1.0 - sigmoid)))).astype(bf16)
    up_low = (hidden_grad * (gate_rows * sigmoid)).astype(bf16)
    two_part = jnp.concatenate(
        [
            (times_t(gate_low, g) + times_t(up_low, u)).astype(bf16)
            for g, u in zip(gate_full, up_full)
        ],
        axis=1,
    )
    normed_two_grad = ffn_to_near(scatter_tokens(two_part, "fsdp"))
    gain_two_grad = jnp.sum(normed_two_grad * unit_two, axis=0)
    middle_grad = plain_to_near(grad_own).astype(f32) + normalize_back(
        normed_two_grad * gain_two, unit_two, inverse_two
    )
    ffn_grads = [
        jnp.concatenate(
            [
                t_times(n, gate_low).astype(bf16),
                t_times(n, up_low).astype(bf16),
                t_times(g, hidden_units).astype(bf16),
            ],
            axis=0,
        )
        for n, g in zip(split(normed_two, n_c, 1), split(grad_rows, n_c, 1))
    ]
    ffn_grad = sum_partners(ffn_grads, "ctx").astype(bf16)
    by_owner = [
        jnp.concatenate(parts, axis=0)
        for parts in zip(*[split(g, n_z, 0) for g in split(ffn_grad, 3, 0)])
    ]
    arrived = [split(b, 3, 0) for b in exchange(by_owner, "fsdp")]
    grad_gate, grad_up, grad_down_t = [
        jnp.concatenate([b[w] for b in arrived], axis=1).astype(f32) for w in range(3)
    ]

    branch_grad = gather_tokens(middle_grad.astype(bf16), "ctx")
    headed_grad = sum_times(branch_grad, out_full)
    scaled_grad = headed_grad * (1.0 - lambda_init)
    head_gain_grad = jnp.sum(scaled_grad * unit_head, axis=0)
    attended_grad = normalize_back(scaled_grad * head_gain, unit_head, inverse_head).astype(bf16)
    mix_grad = times_t(attended_grad, value_rows)
    first_sum = jnp.sum(shares[0] * mix_grad, axis=-1, keepdims=True)
    second_sum = jnp.sum(shares[1] * mix_grad, axis=-1, keepdims=True)
    score_grads = [
        (shares[0] * (mix_grad - first_sum)).astype(bf16),
        (-weight_lambda * shares[1] * (mix_grad - second_sum)).astype(bf16),
    ]
    value_grad = t_times(mix, attended_grad)
    query_grad = jnp.concatenate([times(s, k) for s, k in zip(score_grads, keys)], axis=1)
    key_grad = jnp.concatenate([t_times(s, q) for s, q in zip(score_grads, queries)], axis=1)
    qkv_low = jnp.concatenate(
        [
            rotate_maps(query_grad * scaling, -sine).astype(bf16),
            rotate_maps(key_grad * scaling, -sine).astype(bf16),
            value_grad.astype(bf16),
        ],
        axis=1,
    )
    qkv_grad = sum_partners(
        [t_times(n, qkv_low).astype(bf16) for n in split(normed_one, n_z, 1)], "fsdp"
    )
    out_grad = sum_partners(
        [t_times(b, headed).astype(bf16) for b in split(branch_grad, n_z, 1)], "fsdp"
    )
    qkv_cols = exchange(split(qkv_grad.astype(bf16), n_c, 0), "ctx")
    out_cols = exchange(split(out_grad.astype(bf16), n_c, 0), "ctx")
    edges = (0, 2 * qk_width, 4 * qk_width, 4 * qk_width + value_width)
    grad_query, grad_key, grad_value = [
        jnp.concatenate([b[:, lo:hi] for b in qkv_cols], axis=1).astype(f32)
        for lo, hi in zip(edges[:-1], edges[1:])
    ]
    grad_out = jnp.concatenate(out_cols, axis=1).astype(f32).T
    one_part = jnp.concatenate([times_t(qkv_low, b).astype(bf16) for b in qkv_full], axis=1)
    normed_one_grad = scatter_tokens(one_part, "ctx")
    gain_one_grad = jnp.sum(normed_one_grad * unit_one, axis=0)
    grad_own_in = middle_grad + normalize_back(normed_one_grad * gain_one, unit_one, inverse_one)
    input_grad = plain_to_near(grad_own_in).astype(bf16)

    def both_halves(v):
        other = partner(v, "tp", 1)
        return jnp.concatenate(
            [jnp.where(core == 0, v, other), jnp.where(core == 0, other, v)], axis=0
        )

    sums = jnp.concatenate(
        [
            plain_to_near(gain_one_grad[None])[0],
            plain_to_near(gain_two_grad[None])[0],
            head_gain_grad,
            jnp.full((qk_width,), jnp.sum(second_sum)),
        ]
    )
    for axis in ("tp", "ctx", "fsdp"):
        bit = 1
        while bit < lax.axis_size(axis):
            sums = sums + partner(sums, axis, bit)
            bit *= 2
    at = (z * n_c + c) * piece
    grad_norm_gain = lax.dynamic_slice_in_dim(sums, at, piece)
    grad_ffn_gain = lax.dynamic_slice_in_dim(sums, width + at, piece)
    grad_head_gain = sums[2 * width : 2 * width + value_width]
    lambda_scalar = -sums[2 * width + value_width]
    grad_lambdas = lambda_scalar * jnp.stack(
        [
            first_exp * lambdas[1],
            first_exp * lambdas[0],
            -second_exp * lambdas[3],
            -second_exp * lambdas[2],
        ]
    )
    return (
        both_halves(result)[None],
        both_halves(input_grad)[None],
        grad_norm_gain,
        grad_query,
        grad_key,
        grad_value,
        grad_out,
        grad_lambdas,
        grad_head_gain,
        grad_ffn_gain,
        grad_gate,
        grad_up,
        grad_down_t.T,
    )


def solution(mesh):
    placed = (
        P("fsdp", "ctx", None),
        P("fsdp", "ctx"),
        P("fsdp", "ctx"),
        P(("fsdp", "ctx")),
        P(("fsdp", "ctx"), "tp"),
        P(("fsdp", "ctx"), "tp"),
        P(("fsdp", "ctx"), "tp"),
        P("tp", ("fsdp", "ctx")),
        P(),
        P(),
        P(("fsdp", "ctx")),
        P(("fsdp", "ctx"), "tp"),
        P(("fsdp", "ctx"), "tp"),
        P("tp", ("fsdp", "ctx")),
        P("fsdp", "ctx", None),
    )
    return jax.shard_map(
        by_head if fits_by_head(mesh.shape) else shards,
        mesh=mesh,
        in_specs=placed,
        out_specs=(
            P("fsdp", "ctx", None),
            P("fsdp", "ctx", None),
            P(("fsdp", "ctx")),
            P(("fsdp", "ctx"), "tp"),
            P(("fsdp", "ctx"), "tp"),
            P(("fsdp", "ctx"), "tp"),
            P("tp", ("fsdp", "ctx")),
            P(),
            P(),
            P(("fsdp", "ctx")),
            P(("fsdp", "ctx"), "tp"),
            P(("fsdp", "ctx"), "tp"),
            P("tp", ("fsdp", "ctx")),
        ),
        check_vma=False,
    )
```
